512 devices in a mesh: grid: 64 (over x, y_hi, z), orb: 8 (over y_lo, core).
Axes of the slice: x: 4, y: 8 (y_hi: 2, y_lo: 4; y = y_hi * 4 + y_lo), z: 8, core: 2. Of those that a mesh axis runs over, the one named last changes fastest.
Arguments:
- orbitals: float32 [32, 1024, 32, 256], P('orb', 'grid'), may hold values from -6 to 6
- potential: float32 [1024, 32, 256], P('grid'), may hold values from -1 to 1
- lower_cut: float32 [1], replicated, may hold values from 0.5 to 1.5
- upper_bound: float32 [1], replicated, may hold values from 11 to 12
- rotation: float32 [32, 16], P('orb'), may hold values from -1 to 1
Outputs:
- filtered: float32 [32, 1024, 32, 256], P('orb', 'grid')
- rotated: float32 [16, 1024, 32, 256], P(None, 'grid', 'orb')
The draws below stay inside these ranges and needn't reach their ends.
All inputs are finite; a program needn't handle non-finite values.
Results may differ from the reference program's by a relative error of at most 0.00011.
Values sent between devices are 32-bit elements; how exact they have to be, the bound alone decides.
No kernel may reach another device: no remote copies, remote signals or barrier semaphores. Data moves between devices by JAX's collectives and lax.ppermute only.
A program may use at most 64 MiB of HBM per device.

```python
import jax
import jax.numpy as jnp
from jax import lax

BLOCK = 32
R = 2
NX = 256
NY = 32
NCOL = 16
NZ = 1024


def steps_of(own_key, dims, cuts, smallest, top_value):
    def one(axis_at, shards_of):
        steps = jax.random.uniform(jax.random.fold_in(jax.random.fold_in(own_key, 6), axis_at), (shards_of,), jnp.float32, smallest / len(cuts), top_value / len(cuts))
        return jnp.repeat(jnp.exp(steps), dims[axis_at] // shards_of).reshape((-1,) + (1,) * (len(dims) - axis_at - 1))

    factor_of = one(*cuts[0])
    for cut in cuts[1:]:
        factor_of = factor_of * one(*cut)
    return factor_of


def centred(rng, dims, scale, reach, split=(), held_as=jnp.bfloat16):
    entries = jax.random.normal(rng, dims, jnp.float32) * scale
    if len(split) > 0:
        entries = steps_of(rng, dims, split, -0.22, 0.18) * entries
    return jnp.clip(entries, min=-reach, max=reach).astype(held_as)


def setup_inputs(seed: int = 0) -> dict:
    streams_of = jax.random.split(jax.random.key(seed), 6)
    orbitals = centred(streams_of[0], (BLOCK, NZ, NY, NX), 1.0, 6.0, ((0, 8), (1, 64)), jnp.float32)
    potential = jnp.clip(jax.random.uniform(streams_of[1], (NZ, NY, NX), jnp.float32, -1.0, 1.0) * steps_of(streams_of[1], (NZ, NY, NX), ((0, 64),), -0.4, 0.0), -1.0, 1.0)
    lower_cut = jnp.clip(jax.random.uniform(streams_of[2], (1,), jnp.float32, 0.5, 1.5), 0.5, 1.5)
    upper_bound = jnp.clip(jax.random.uniform(streams_of[3], (1,), jnp.float32, 11.0, 12.0), 11.0, 12.0)
    rotation = centred(streams_of[4], (BLOCK, NCOL), BLOCK ** -0.5, 1.0, ((0, 8),), jnp.float32)
    return {"orbitals": orbitals, "potential": potential, "lower_cut": lower_cut, "upper_bound": upper_bound, "rotation": rotation}


STENCIL_WEIGHTS = (-5.0 / 2.0, 4.0 / 3.0, -1.0 / 12.0)
SPACING = 1.0


def laplace(field):
    summed = 3.0 * STENCIL_WEIGHTS[0] * field
    for offset in range(1, R + 1):
        beside_all = jnp.roll(field, offset, 0) + jnp.roll(field, -offset, 0)
        beside_all = beside_all + jnp.roll(field, offset, 1) + jnp.roll(field, -offset, 1)
        beside_all = beside_all + jnp.roll(field, offset, 2) + jnp.roll(field, -offset, 2)
        summed = summed + STENCIL_WEIGHTS[offset] * beside_all
    return summed


def reference(orbitals, potential, lower_cut, upper_bound, rotation):
    middle = (upper_bound[0] + lower_cut[0]) * 0.5
    half_width = (upper_bound[0] - lower_cut[0]) * 0.5

    def hamilton(field):
        return -0.5 * laplace(field) / (SPACING * SPACING) + potential * field

    def filter_one(start):
        first = (hamilton(start) - middle * start) / half_width
        return 2.0 * (hamilton(first) - middle * first) / half_width - start

    filtered = lax.map(filter_one, orbitals)
    flat = filtered.reshape(BLOCK, NZ * NY * NX)
    rotated = jnp.dot(rotation.T, flat, precision=lax.Precision.HIGHEST, preferred_element_type=jnp.float32)
    return filtered, rotated.reshape(NCOL, NZ, NY, NX)
```

```python
import jax
import jax.numpy as jnp
from jax import lax
from jax.experimental import pallas as pl
from jax.experimental.pallas import tpu as pltpu
from jax.sharding import PartitionSpec as P

W0, W1, W2 = -5.0 / 2.0, 4.0 / 3.0, -1.0 / 12.0
F32 = jnp.float32
ORBS, PLANES, ROWS, COLS = 4, 16, 32, 256
REACH = 4
PEERS, NCOL = 8, 16
LIMIT = 48 * 1024 * 1024


def coefficients(lower_ref, upper_ref):
    middle = (upper_ref[0] + lower_ref[0]) * 0.5
    inverse = 1.0 / ((upper_ref[0] - lower_ref[0]) * 0.5)
    return (-1.5 * W0 - middle) * inverse, inverse, -0.5 * W1 * inverse


def scaled_hamilton(planes, local, coef):
    base, inverse, near = coef
    below2, below1, f, above1, above2 = planes
    s1 = below1 + above1
    s2 = below2 + above2
    s1 = s1 + (pltpu.roll(f, 1, 0) + pltpu.roll(f, ROWS - 1, 0))
    s2 = s2 + (pltpu.roll(f, 2, 0) + pltpu.roll(f, ROWS - 2, 0))
    s1 = s1 + (pltpu.roll(f, 1, 1) + pltpu.roll(f, COLS - 1, 1))
    s2 = s2 + (pltpu.roll(f, 2, 1) + pltpu.roll(f, COLS - 2, 1))
    return f * (base + inverse * local) + near * (s1 + (W2 / W1) * s2)


def first_planes(count, source, local, store, coef):
    def step(p, carry):
        store(p, scaled_hamilton([source(p + d) for d in range(5)], local(p), coef))
        return carry

    lax.fori_loop(0, count, step, 0, unroll=2)


def filtered_plane(q, first, original, local, coef):
    g = scaled_hamilton([first(q + d) for d in range(5)], local, coef)
    return 2.0 * g - original


def pack_pair(mine, slots_ref, row, g0, g1):
    low = lax.broadcasted_iota(jnp.int32, (8, 128), 0) < 4
    for k in range(ROWS // 8):
        for h in range(COLS // 128):
            a = g0[8 * k : 8 * k + 8, 128 * h : 128 * h + 128]
            b = g1[8 * k : 8 * k + 8, 128 * h : 128 * h + 128]
            at = slice(row + 8 * h, row + 8 * h + 8)
            slots_ref[jnp.bitwise_xor(mine, 2 * k), at, :] = jnp.where(low, a, pltpu.roll(b, 4, 0))
            slots_ref[jnp.bitwise_xor(mine, 2 * k + 1), at, :] = jnp.where(
                low, pltpu.roll(a, 4, 0), b
            )


def inner_kernel(
    lower_ref, upper_ref, orb_ref, pot_ref, rot_ref, out_ref, first_ref, send_ref, slots_ref
):
    coef = coefficients(lower_ref, upper_ref)
    orbital = pl.program_id(0)

    def store(p, value):
        first_ref[0, p] = value

    first_planes(12, lambda p: orb_ref[0, p], lambda p: pot_ref[p + 2], store, coef)
    for t in range(4):
        pair = []
        for q in (2 * t, 2 * t + 1):
            g = filtered_plane(
                q, lambda p: first_ref[0, p], orb_ref[0, q + 4], pot_ref[q + 4], coef
            )
            out_ref[0, q + 4] = g
            pair.append(g)
        pack_pair(0, slots_ref, t * 16, *pair)
    for slot in range(PEERS):
        send_ref[slot, pl.ds(pl.multiple_of(orbital * 64, 64), 64), :] = slots_ref[slot]
        send_ref[slot, 256:264, :] = rot_ref[...]


def outer_kernel(
    mine_ref, lower_ref, upper_ref, orb_ref, pot_ref, stored_ref, low_ref, low_pot_ref,
    high_ref, high_pot_ref, _, *rest,
):
    out_ref, sends, (ext_ref, local_ref, first_ref, slots_ref) = rest[0], rest[1:-4], rest[-4:]
    coef = coefficients(lower_ref, upper_ref)
    mine, side = mine_ref[0], pl.program_id(1)

    @pl.when(side == 0)
    def _():
        ext_ref[0:4] = low_ref[...]
        ext_ref[4:8] = orb_ref[0]
        local_ref[0:2] = low_pot_ref[...]
        local_ref[2:4] = pot_ref[0:2]
        first_ref[4:8] = stored_ref[0]

    @pl.when(side == 1)
    def _():
        ext_ref[0:4] = orb_ref[0]
        ext_ref[4:8] = high_ref[...]
        local_ref[0:2] = pot_ref[14:16]
        local_ref[2:4] = high_pot_ref[...]
        first_ref[0:4] = stored_ref[0]

    def store(p, value):
        first_ref[4 * side + p] = value

    first_planes(4, lambda p: ext_ref[p], lambda p: local_ref[p], store, coef)
    for t in range(2):
        pair = []
        for q in (2 * t, 2 * t + 1):
            g = filtered_plane(
                q, lambda p: first_ref[p], ext_ref[q + 4 - 4 * side], pot_ref[q + 12 * side], coef
            )
            out_ref[0, q] = g
            pair.append(g)
        pack_pair(mine, slots_ref, t * 16, *pair)
    for slot, send_ref in enumerate(sends):
        send_ref[...] = slots_ref[slot]


def rotate_tiles(u, tile, weight, out_ref):
    width = 8
    for first in range(0, NCOL, width):
        sums = [jnp.zeros((8, 128), F32)] * (4 * width)
        for slot in range(PEERS):
            for i in range(ORBS):
                rows = [pl.multiple_of(i * 64 + u * 32 + 8 * n, 8) for n in range(4)]
                values = [tile(slot, pl.ds(row, 8)) for row in rows]
                for j in range(width):
                    factor = weight(slot, i * NCOL + first + j)
                    for n in range(4):
                        sums[4 * j + n] = sums[4 * j + n] + factor * values[n]
        for j in range(width):
            for n in range(4):
                t, h = divmod(n, 2)
                columns = slice(128 * h, 128 * h + 128)
                out_ref[first + j, 2 * t, :, columns] = sums[4 * j + n][0:4]
                out_ref[first + j, 2 * t + 1, :, columns] = sums[4 * j + n][4:8]


def rotate_inner_kernel(rot_ref, recv_ref, out_ref):
    rotate_tiles(
        pl.program_id(0),
        lambda slot, rows: recv_ref[slot, rows, :],
        lambda slot, n: rot_ref[slot, n],
        out_ref,
    )


def rotate_outer_kernel(mine_ref, rot_ref, *rest):
    received, out_ref, mine = rest[:PEERS], rest[-1], mine_ref[0]
    rotate_tiles(
        pl.program_id(0),
        lambda slot, rows: received[slot][rows, :],
        lambda slot, n: rot_ref[jnp.bitwise_xor(mine, slot), n],
        out_ref,
    )


SMEM = pl.BlockSpec(memory_space=pltpu.SMEM)
ANY = pl.BlockSpec(memory_space=pl.ANY)


def params():
    return pltpu.CompilerParams(vmem_limit_bytes=LIMIT)


def cost(flops, moved):
    return pl.CostEstimate(flops=flops, bytes_accessed=moved, transcendentals=0)


def body(orbitals, potential, lower_cut, upper_bound, rotation):
    count = lax.axis_size("grid")
    forward = [(i, (i + 1) % count) for i in range(count)]
    backward = [(target, source) for source, target in forward]
    plane = (ROWS, COLS)

    def packed(first_plane, first_local):
        own = orbitals[:, first_plane : first_plane + REACH].reshape((ORBS * REACH,) + plane)
        return jnp.concatenate([own, potential[first_local : first_local + 2]], axis=0)

    low = lax.ppermute(packed(PLANES - REACH, PLANES - 2), "grid", forward)
    high = lax.ppermute(packed(0, 0), "grid", backward)

    orb_hbm = pltpu.with_memory_space_constraint(orbitals, pltpu.HBM)
    pot_hbm = pltpu.with_memory_space_constraint(potential, pltpu.HBM)
    rot_tile = jnp.pad(rotation.reshape(1, ORBS * NCOL), ((0, 7), (0, 128 - ORBS * NCOL)))
    mine = lax.axis_index("orb").astype(jnp.int32).reshape(1)
    filtered_shape = pltpu.HBM((ORBS, PLANES) + plane, F32)

    def regroup(sends):
        got = [sends[0]] + [None] * (PEERS - 1)
        for k in (4, 5, 6, 7, 2, 3, 1):
            got[k] = lax.ppermute(sends[k], "orb", [(o, o ^ k) for o in range(PEERS)])
        return got

    filtered, stored, send = pl.pallas_call(
        inner_kernel,
        grid=(ORBS,),
        in_specs=[
            SMEM,
            SMEM,
            pl.BlockSpec((1, PLANES) + plane, lambda i: (i, 0, 0, 0)),
            pl.BlockSpec((PLANES,) + plane, lambda i: (0, 0, 0)),
            pl.BlockSpec((8, 128), lambda i: (0, 0)),
        ],
        out_specs=[
            pl.BlockSpec((1, PLANES) + plane, lambda i: (i, 0, 0, 0)),
            pl.BlockSpec((1, 12) + plane, lambda i: (i, 0, 0, 0)),
            pl.BlockSpec((PEERS, 264, 128), lambda i: (0, 0, 0)),
        ],
        out_shape=[
            filtered_shape,
            pltpu.HBM((ORBS, 12) + plane, F32),
            pltpu.HBM((PEERS, 264, 128), F32),
        ],
        scratch_shapes=[pltpu.VMEM((PEERS, 64, 128), F32)],
        compiler_params=params(),
        cost_estimate=cost(1_000_000, 1_000_000),
        name="filter_inner",
    )(lower_cut, upper_bound, orb_hbm, pot_hbm, rot_tile)
    received = lax.all_to_all(send, "orb", split_axis=0, concat_axis=0, tiled=True)
    stored = pltpu.with_memory_space_constraint(stored, pltpu.HBM)

    filtered, *sends_outer = pl.pallas_call(
        outer_kernel,
        grid=(ORBS, 2),
        in_specs=[
            SMEM,
            SMEM,
            SMEM,
            pl.BlockSpec((1, 4) + plane, lambda i, s: (i, 3 * s, 0, 0)),
            pl.BlockSpec((PLANES,) + plane, lambda i, s: (0, 0, 0)),
            pl.BlockSpec((1, 4) + plane, lambda i, s: (i, 2 * s, 0, 0)),
            pl.BlockSpec((4,) + plane, lambda i, s: (i, 0, 0)),
            pl.BlockSpec((2,) + plane, lambda i, s: (8, 0, 0)),
            pl.BlockSpec((4,) + plane, lambda i, s: (i, 0, 0)),
            pl.BlockSpec((2,) + plane, lambda i, s: (8, 0, 0)),
            ANY,
        ],
        out_specs=[pl.BlockSpec((1, 4) + plane, lambda i, s: (i, 3 * s, 0, 0))]
        + [pl.BlockSpec((32, 128), lambda i, s: (2 * i + s, 0))] * PEERS,
        out_shape=[filtered_shape] + [jax.ShapeDtypeStruct((256, 128), F32)] * PEERS,
        scratch_shapes=[
            pltpu.VMEM((8,) + plane, F32),
            pltpu.VMEM((4,) + plane, F32),
            pltpu.VMEM((8,) + plane, F32),
            pltpu.VMEM((PEERS, 32, 128), F32),
        ],
        input_output_aliases={10: 0},
        compiler_params=params(),
        cost_estimate=cost(400_000_000_000, 400_000_000),
        name="filter_outer",
    )(mine, lower_cut, upper_bound, orb_hbm, pot_hbm, stored, low, low, high, high, filtered)
    received_outer = regroup(sends_outer)

    weights = received[:, 256, : ORBS * NCOL]
    rotated_shape = jax.ShapeDtypeStruct((NCOL, PLANES, 4, COLS), F32)
    vmem = pl.BlockSpec(memory_space=pltpu.VMEM)
    rotated = pl.pallas_call(
        rotate_inner_kernel,
        grid=(2,),
        in_specs=[SMEM, vmem],
        out_specs=pl.BlockSpec((NCOL, 4, 4, COLS), lambda u: (0, 1 + u, 0, 0)),
        out_shape=rotated_shape,
        compiler_params=params(),
        cost_estimate=cost(8_000_000, 1_600_000),
        name="rotate_inner",
    )(weights, received)
    rotated = pl.pallas_call(
        rotate_outer_kernel,
        grid=(2,),
        in_specs=[SMEM, SMEM] + [vmem] * PEERS + [ANY],
        out_specs=pl.BlockSpec((NCOL, 4, 4, COLS), lambda u: (0, 3 * u, 0, 0)),
        out_shape=rotated_shape,
        input_output_aliases={PEERS + 2: 0},
        compiler_params=params(),
        cost_estimate=cost(8_000_000, 1_600_000),
        name="rotate_outer",
    )(mine, weights, *received_outer, rotated)
    return (filtered, rotated)


def solution(mesh):
    in_specs = (P("orb", "grid", None, None), P("grid", None, None), P(), P(), P("orb", None))
    out_specs = (P("orb", "grid", None, None), P(None, "grid", "orb", None))
    return jax.shard_map(body, mesh=mesh, in_specs=in_specs, out_specs=out_specs, check_vma=False)
```

```python
import jax
import jax.numpy as jnp
from jax import lax
from jax.experimental import pallas as pl
from jax.experimental.pallas import tpu as pltpu
from jax.sharding import PartitionSpec as P

W0, W1, W2 = -5.0 / 2.0, 4.0 / 3.0, -1.0 / 12.0
F32 = jnp.float32
ORBS, PLANES, ROWS, COLS = 4, 16, 32, 256
REACH = 4
PEERS, NCOL = 8, 16
LIMIT = 48 * 1024 * 1024
ORDER = (4, 5, 6, 7, 2, 3, 1, 0)


def coefficients(lower_ref, upper_ref):
    middle = (upper_ref[0] + lower_ref[0]) * 0.5
    inverse = 1.0 / ((upper_ref[0] - lower_ref[0]) * 0.5)
    return (-1.5 * W0 - middle) * inverse, inverse, -0.5 * W1 * inverse


def scaled_hamilton(planes, local, coef):
    base, inverse, near = coef
    below2, below1, f, above1, above2 = planes
    s1 = below1 + above1
    s2 = below2 + above2
    s1 = s1 + (pltpu.roll(f, 1, 0) + pltpu.roll(f, ROWS - 1, 0))
    s2 = s2 + (pltpu.roll(f, 2, 0) + pltpu.roll(f, ROWS - 2, 0))
    s1 = s1 + (pltpu.roll(f, 1, 1) + pltpu.roll(f, COLS - 1, 1))
    s2 = s2 + (pltpu.roll(f, 2, 1) + pltpu.roll(f, COLS - 2, 1))
    return f * (base + inverse * local) + near * (s1 + (W2 / W1) * s2)


def first_planes(count, source, local, store, coef):
    def step(p, carry):
        store(p, scaled_hamilton([source(p + d) for d in range(5)], local(p), coef))
        return carry

    lax.fori_loop(0, count, step, 0, unroll=2)


def filtered_plane(q, first, original, local, coef):
    g = scaled_hamilton([first(q + d) for d in range(5)], local, coef)
    return 2.0 * g - original


def pack_pair(mine, slots_ref, row, g0, g1):
    low = lax.broadcasted_iota(jnp.int32, (8, 128), 0) < 4
    for k in range(ROWS // 8):
        for h in range(COLS // 128):
            a = g0[8 * k : 8 * k + 8, 128 * h : 128 * h + 128]
            b = g1[8 * k : 8 * k + 8, 128 * h : 128 * h + 128]
            at = slice(row + 8 * h, row + 8 * h + 8)
            slots_ref[jnp.bitwise_xor(mine, 2 * k), at, :] = jnp.where(low, a, pltpu.roll(b, 4, 0))
            slots_ref[jnp.bitwise_xor(mine, 2 * k + 1), at, :] = jnp.where(
                low, pltpu.roll(a, 4, 0), b
            )


def inner_kernel(
    lower_ref, upper_ref, orb_ref, pot_ref, rot_ref, out_ref, first_ref, send_ref, slots_ref
):
    coef = coefficients(lower_ref, upper_ref)
    orbital = pl.program_id(0)

    def store(p, value):
        first_ref[0, p] = value

    first_planes(12, lambda p: orb_ref[0, p], lambda p: pot_ref[p + 2], store, coef)
    for t in range(4):
        pair = []
        for q in (2 * t, 2 * t + 1):
            g = filtered_plane(
                q, lambda p: first_ref[0, p], orb_ref[0, q + 4], pot_ref[q + 4], coef
            )
            out_ref[0, q + 4] = g
            pair.append(g)
        pack_pair(0, slots_ref, t * 16, *pair)
    for slot in range(PEERS):
        send_ref[slot, pl.ds(pl.multiple_of(orbital * 64, 64), 64), :] = slots_ref[slot]
        send_ref[slot, 256:264, :] = rot_ref[...]


def outer_kernel(
    mine_ref, lower_ref, upper_ref, orb_ref, pot_ref, stored_ref, low_ref, low_pot_ref,
    high_ref, high_pot_ref, _, *rest,
):
    out_ref, sends, (ext_ref, local_ref, first_ref, slots_ref) = rest[0], rest[1:-4], rest[-4:]
    coef = coefficients(lower_ref, upper_ref)
    mine, side = mine_ref[0], pl.program_id(1)

    @pl.when(side == 0)
    def _():
        ext_ref[0:4] = low_ref[...]
        ext_ref[4:8] = orb_ref[0]
        local_ref[0:2] = low_pot_ref[...]
        local_ref[2:4] = pot_ref[0:2]
        first_ref[4:8] = stored_ref[0]

    @pl.when(side == 1)
    def _():
        ext_ref[0:4] = orb_ref[0]
        ext_ref[4:8] = high_ref[...]
        local_ref[0:2] = pot_ref[14:16]
        local_ref[2:4] = high_pot_ref[...]
        first_ref[0:4] = stored_ref[0]

    def store(p, value):
        first_ref[4 * side + p] = value

    first_planes(4, lambda p: ext_ref[p], lambda p: local_ref[p], store, coef)
    for t in range(2):
        pair = []
        for q in (2 * t, 2 * t + 1):
            g = filtered_plane(
                q, lambda p: first_ref[p], ext_ref[q + 4 - 4 * side], pot_ref[q + 12 * side], coef
            )
            out_ref[0, q] = g
            pair.append(g)
        pack_pair(mine, slots_ref, t * 16, *pair)
    for slot, send_ref in enumerate(sends):
        send_ref[...] = slots_ref[slot]


def rotate_tiles(u, tile, weight, out_ref):
    width = 8
    for first in range(0, NCOL, width):
        sums = [jnp.zeros((8, 128), F32)] * (4 * width)
        for slot in range(PEERS):
            for i in range(ORBS):
                rows = [pl.multiple_of(i * 64 + u * 32 + 8 * n, 8) for n in range(4)]
                values = [tile(slot, pl.ds(row, 8)) for row in rows]
                for j in range(width):
                    factor = weight(slot, i * NCOL + first + j)
                    for n in range(4):
                        sums[4 * j + n] = sums[4 * j + n] + factor * values[n]
        for j in range(width):
            for n in range(4):
                t, h = divmod(n, 2)
                columns = slice(128 * h, 128 * h + 128)
                out_ref[first + j, 2 * t, :, columns] = sums[4 * j + n][0:4]
                out_ref[first + j, 2 * t + 1, :, columns] = sums[4 * j + n][4:8]


def rotate_inner_kernel(rot_ref, recv_ref, out_ref):
    rotate_tiles(
        pl.program_id(0),
        lambda slot, rows: recv_ref[slot, rows, :],
        lambda slot, n: rot_ref[slot, n],
        out_ref,
    )


def rotate_outer_kernel(mine_ref, rot_ref, *rest):
    received, out_ref, mine = rest[:PEERS], rest[-1], mine_ref[0]
    rotate_tiles(
        pl.program_id(0),
        lambda slot, rows: received[slot][rows, :],
        lambda slot, n: rot_ref[jnp.bitwise_xor(mine, ORDER[slot]), n],
        out_ref,
    )


SMEM = pl.BlockSpec(memory_space=pltpu.SMEM)
ANY = pl.BlockSpec(memory_space=pl.ANY)


def params():
    return pltpu.CompilerParams(vmem_limit_bytes=LIMIT)


def cost(flops, moved):
    return pl.CostEstimate(flops=flops, bytes_accessed=moved, transcendentals=0)


def body(orbitals, potential, lower_cut, upper_bound, rotation):
    count = lax.axis_size("grid")
    forward = [(i, (i + 1) % count) for i in range(count)]
    backward = [(target, source) for source, target in forward]
    plane = (ROWS, COLS)

    def packed(first_plane, first_local):
        own = orbitals[:, first_plane : first_plane + REACH].reshape((ORBS * REACH,) + plane)
        return jnp.concatenate([own, potential[first_local : first_local + 2]], axis=0)

    low = lax.ppermute(packed(PLANES - REACH, PLANES - 2), "grid", forward)
    high = lax.ppermute(packed(0, 0), "grid", backward)

    rot_tile = jnp.pad(rotation.reshape(1, ORBS * NCOL), ((0, 7), (0, 128 - ORBS * NCOL)))
    mine = lax.axis_index("orb").astype(jnp.int32).reshape(1)
    filtered_shape = pltpu.HBM((ORBS, PLANES) + plane, F32)

    def regroup(sends):
        return [
            lax.ppermute(sends[k], "orb", [(o, o ^ k) for o in range(PEERS)]) if k else sends[k]
            for k in ORDER
        ]

    filtered, stored, send = pl.pallas_call(
        inner_kernel,
        grid=(ORBS,),
        in_specs=[
            SMEM,
            SMEM,
            pl.BlockSpec((1, PLANES) + plane, lambda i: (i, 0, 0, 0)),
            pl.BlockSpec((PLANES,) + plane, lambda i: (0, 0, 0)),
            pl.BlockSpec((8, 128), lambda i: (0, 0)),
        ],
        out_specs=[
            pl.BlockSpec((1, PLANES) + plane, lambda i: (i, 0, 0, 0)),
            pl.BlockSpec((1, 12) + plane, lambda i: (i, 0, 0, 0)),
            pl.BlockSpec((PEERS, 264, 128), lambda i: (0, 0, 0)),
        ],
        out_shape=[
            filtered_shape,
            jax.ShapeDtypeStruct((ORBS, 12) + plane, F32),
            pltpu.HBM((PEERS, 264, 128), F32),
        ],
        scratch_shapes=[pltpu.VMEM((PEERS, 64, 128), F32)],
        compiler_params=params(),
        cost_estimate=cost(1_000_000, 1_000_000),
        name="filter_inner",
    )(lower_cut, upper_bound, orbitals, potential, rot_tile)
    received = lax.all_to_all(send, "orb", split_axis=0, concat_axis=0, tiled=True)

    filtered, *sends_outer = pl.pallas_call(
        outer_kernel,
        grid=(ORBS, 2),
        in_specs=[
            SMEM,
            SMEM,
            SMEM,
            pl.BlockSpec((1, 4) + plane, lambda i, s: (i, 3 * s, 0, 0)),
            pl.BlockSpec((PLANES,) + plane, lambda i, s: (0, 0, 0)),
            pl.BlockSpec((1, 4) + plane, lambda i, s: (i, 2 * s, 0, 0)),
            pl.BlockSpec((4,) + plane, lambda i, s: (i, 0, 0)),
            pl.BlockSpec((2,) + plane, lambda i, s: (8, 0, 0)),
            pl.BlockSpec((4,) + plane, lambda i, s: (i, 0, 0)),
            pl.BlockSpec((2,) + plane, lambda i, s: (8, 0, 0)),
            ANY,
        ],
        out_specs=[pl.BlockSpec((1, 4) + plane, lambda i, s: (i, 3 * s, 0, 0))]
        + [pl.BlockSpec((32, 128), lambda i, s: (2 * i + s, 0))] * PEERS,
        out_shape=[filtered_shape] + [jax.ShapeDtypeStruct((256, 128), F32)] * PEERS,
        scratch_shapes=[
            pltpu.VMEM((8,) + plane, F32),
            pltpu.VMEM((4,) + plane, F32),
            pltpu.VMEM((8,) + plane, F32),
            pltpu.VMEM((PEERS, 32, 128), F32),
        ],
        input_output_aliases={10: 0},
        compiler_params=params(),
        cost_estimate=cost(400_000_000_000, 400_000_000),
        name="filter_outer",
    )(mine, lower_cut, upper_bound, orbitals, potential, stored, low, low, high, high, filtered)
    received_outer = regroup(sends_outer)

    weights = received[:, 256, : ORBS * NCOL]
    rotated_shape = jax.ShapeDtypeStruct((NCOL, PLANES, 4, COLS), F32)
    vmem = pl.BlockSpec(memory_space=pltpu.VMEM)
    rotated = pl.pallas_call(
        rotate_inner_kernel,
        grid=(2,),
        in_specs=[SMEM, vmem],
        out_specs=pl.BlockSpec((NCOL, 4, 4, COLS), lambda u: (0, 1 + u, 0, 0)),
        out_shape=rotated_shape,
        compiler_params=params(),
        cost_estimate=cost(8_000_000, 1_600_000),
        name="rotate_inner",
    )(weights, received)
    rotated = pl.pallas_call(
        rotate_outer_kernel,
        grid=(2,),
        in_specs=[SMEM, SMEM] + [vmem] * PEERS + [ANY],
        out_specs=pl.BlockSpec((NCOL, 4, 4, COLS), lambda u: (0, 3 * u, 0, 0)),
        out_shape=rotated_shape,
        input_output_aliases={PEERS + 2: 0},
        compiler_params=params(),
        cost_estimate=cost(8_000_000, 1_600_000),
        name="rotate_outer",
    )(mine, weights, *received_outer, rotated)
    return (filtered, rotated)


def solution(mesh):
    in_specs = (P("orb", "grid", None, None), P("grid", None, None), P(), P(), P("orb", None))
    out_specs = (P("orb", "grid", None, None), P(None, "grid", "orb", None))
    return jax.shard_map(body, mesh=mesh, in_specs=in_specs, out_specs=out_specs, check_vma=False)
```

```python
import jax
import jax.numpy as jnp
from jax import lax
from jax.experimental import pallas as pl
from jax.experimental.pallas import tpu as pltpu
from jax.sharding import PartitionSpec as P

W0, W1, W2 = -5.0 / 2.0, 4.0 / 3.0, -1.0 / 12.0
F32 = jnp.float32
ORBS, PLANES, ROWS, COLS = 4, 16, 32, 256
REACH = 4
PEERS, NCOL = 8, 16
LIMIT = 20 * 1024 * 1024
ORDER = (1, 2, 4, 5, 6, 7, 3, 0)


def coefficients(lower_ref, upper_ref):
    middle = (upper_ref[0] + lower_ref[0]) * 0.5
    inverse = 1.0 / ((upper_ref[0] - lower_ref[0]) * 0.5)
    return (-1.5 * W0 - middle) * inverse, inverse, -0.5 * W1 * inverse


def scaled_hamilton(planes, local, coef):
    base, inverse, near = coef
    below2, below1, f, above1, above2 = planes
    s1 = below1 + above1
    s2 = below2 + above2
    s1 = s1 + (pltpu.roll(f, 1, 0) + pltpu.roll(f, ROWS - 1, 0))
    s2 = s2 + (pltpu.roll(f, 2, 0) + pltpu.roll(f, ROWS - 2, 0))
    s1 = s1 + (pltpu.roll(f, 1, 1) + pltpu.roll(f, COLS - 1, 1))
    s2 = s2 + (pltpu.roll(f, 2, 1) + pltpu.roll(f, COLS - 2, 1))
    return f * (base + inverse * local) + near * (s1 + (W2 / W1) * s2)


def first_planes(count, source, local, store, coef):
    def step(p, carry):
        store(p, scaled_hamilton([source(p + d) for d in range(5)], local(p), coef))
        return carry

    lax.fori_loop(0, count, step, 0, unroll=2)


def filtered_plane(q, first, original, local, coef):
    g = scaled_hamilton([first(q + d) for d in range(5)], local, coef)
    return 2.0 * g - original


def pack_pair(mine, slots_ref, row, g0, g1):
    low = lax.broadcasted_iota(jnp.int32, (8, 128), 0) < 4
    for k in range(ROWS // 8):
        for h in range(COLS // 128):
            a = g0[8 * k : 8 * k + 8, 128 * h : 128 * h + 128]
            b = g1[8 * k : 8 * k + 8, 128 * h : 128 * h + 128]
            at = slice(row + 8 * h, row + 8 * h + 8)
            slots_ref[jnp.bitwise_xor(mine, 2 * k), at, :] = jnp.where(low, a, pltpu.roll(b, 4, 0))
            slots_ref[jnp.bitwise_xor(mine, 2 * k + 1), at, :] = jnp.where(
                low, pltpu.roll(a, 4, 0), b
            )


def inner_kernel(
    lower_ref, upper_ref, orb_ref, pot_ref, rot_ref, out_ref, first_ref, send_ref, slots_ref
):
    coef = coefficients(lower_ref, upper_ref)
    orbital = pl.program_id(0)

    def store(p, value):
        first_ref[orbital, p] = value

    first_planes(12, lambda p: orb_ref[orbital, p], lambda p: pot_ref[p + 2], store, coef)
    for t in range(4):
        pair = []
        for q in (2 * t, 2 * t + 1):
            g = filtered_plane(
                q, lambda p: first_ref[orbital, p], orb_ref[orbital, q + 4], pot_ref[q + 4], coef
            )
            out_ref[0, q + 4] = g
            pair.append(g)
        pack_pair(0, slots_ref, t * 16, *pair)
    for slot in range(PEERS):
        send_ref[slot, pl.ds(pl.multiple_of(orbital * 64, 64), 64), :] = slots_ref[slot]
        send_ref[slot, 256:264, :] = rot_ref[...]


def outer_kernel(
    mine_ref, lower_ref, upper_ref, orb_ref, pot_ref, stored_ref, low_ref, high_ref, _, *rest
):
    out_ref, sends, (fresh_ref, slots_ref) = rest[0], rest[1:-2], rest[-2:]
    coef = coefficients(lower_ref, upper_ref)
    mine, i, side = mine_ref[0], pl.program_id(0), pl.program_id(1)
    halo = REACH * i

    def filter_side(raw, local, first, original, own_local):
        for p in range(4):
            fresh_ref[p] = scaled_hamilton([raw(p + d) for d in range(5)], local(p), coef)
        for t in range(2):
            pair = []
            for q in (2 * t, 2 * t + 1):
                g = filtered_plane(q, first, original(q), own_local(q), coef)
                out_ref[0, q] = g
                pair.append(g)
            pack_pair(mine, slots_ref, t * 16, *pair)

    @pl.when(side == 0)
    def _():
        filter_side(
            lambda p: low_ref[halo + p] if p < 4 else orb_ref[i, p - 4],
            lambda p: low_ref[ORBS * REACH + p] if p < 2 else pot_ref[p - 2],
            lambda p: fresh_ref[p] if p < 4 else stored_ref[i, p - 4],
            lambda q: orb_ref[i, q],
            lambda q: pot_ref[q],
        )

    @pl.when(side == 1)
    def _():
        filter_side(
            lambda p: orb_ref[i, 12 + p] if p < 4 else high_ref[halo + p - 4],
            lambda p: pot_ref[14 + p] if p < 2 else high_ref[ORBS * REACH + p - 2],
            lambda p: stored_ref[i, 8 + p] if p < 4 else fresh_ref[p - 4],
            lambda q: orb_ref[i, 12 + q],
            lambda q: pot_ref[12 + q],
        )

    rows = pl.ds(pl.multiple_of((2 * i + side) * 32, 32), 32)
    for slot, send_ref in enumerate(sends):
        send_ref[rows, :] = slots_ref[slot]


def rotate_tiles(u, tile, weight, out_ref):
    width = 8
    for first in range(0, NCOL, width):
        sums = [jnp.zeros((8, 128), F32)] * (4 * width)
        for slot in range(PEERS):
            for i in range(ORBS):
                rows = [pl.multiple_of(i * 64 + u * 32 + 8 * n, 8) for n in range(4)]
                values = [tile(slot, pl.ds(row, 8)) for row in rows]
                for j in range(width):
                    factor = weight(slot, i * NCOL + first + j)
                    for n in range(4):
                        sums[4 * j + n] = sums[4 * j + n] + factor * values[n]
        for j in range(width):
            for n in range(4):
                t, h = divmod(n, 2)
                columns = slice(128 * h, 128 * h + 128)
                out_ref[first + j, 2 * t, :, columns] = sums[4 * j + n][0:4]
                out_ref[first + j, 2 * t + 1, :, columns] = sums[4 * j + n][4:8]


def rotate_inner_kernel(rot_ref, recv_ref, out_ref):
    rotate_tiles(
        pl.program_id(0),
        lambda slot, rows: recv_ref[slot, rows, :],
        lambda slot, n: rot_ref[slot, n],
        out_ref,
    )


def rotate_outer_kernel(mine_ref, rot_ref, *rest):
    received, out_ref, mine = rest[:PEERS], rest[-1], mine_ref[0]
    rotate_tiles(
        pl.program_id(0),
        lambda slot, rows: received[slot][rows, :],
        lambda slot, n: rot_ref[jnp.bitwise_xor(mine, ORDER[slot]), n],
        out_ref,
    )


SMEM = pl.BlockSpec(memory_space=pltpu.SMEM)
VMEM = pl.BlockSpec(memory_space=pltpu.VMEM)
ANY = pl.BlockSpec(memory_space=pl.ANY)


def params():
    return pltpu.CompilerParams(vmem_limit_bytes=LIMIT)


def cost(flops, moved):
    return pl.CostEstimate(flops=flops, bytes_accessed=moved, transcendentals=0)


def body(orbitals, potential, lower_cut, upper_bound, rotation):
    count = lax.axis_size("grid")
    forward = [(i, (i + 1) % count) for i in range(count)]
    backward = [(target, source) for source, target in forward]
    plane = (ROWS, COLS)

    def packed(first_plane, first_local):
        own = orbitals[:, first_plane : first_plane + REACH].reshape((ORBS * REACH,) + plane)
        return jnp.concatenate([own, potential[first_local : first_local + 2]], axis=0)

    low = lax.ppermute(packed(PLANES - REACH, PLANES - 2), "grid", forward)
    high = lax.ppermute(packed(0, 0), "grid", backward)

    rot_tile = jnp.pad(rotation.reshape(1, ORBS * NCOL), ((0, 7), (0, 128 - ORBS * NCOL)))
    mine = lax.axis_index("orb").astype(jnp.int32).reshape(1)
    filtered_shape = pltpu.HBM((ORBS, PLANES) + plane, F32)

    def regroup(sends):
        return [
            lax.ppermute(sends[k], "orb", [(o, o ^ k) for o in range(PEERS)]) if k else sends[k]
            for k in ORDER
        ]

    filtered, stored, send = pl.pallas_call(
        inner_kernel,
        grid=(ORBS,),
        in_specs=[
            SMEM,
            SMEM,
            VMEM,
            VMEM,
            VMEM,
        ],
        out_specs=[
            pl.BlockSpec((1, PLANES) + plane, lambda i: (i, 0, 0, 0)),
            VMEM,
            pl.BlockSpec((PEERS, 264, 128), lambda i: (0, 0, 0)),
        ],
        out_shape=[
            filtered_shape,
            jax.ShapeDtypeStruct((ORBS, 12) + plane, F32),
            pltpu.HBM((PEERS, 264, 128), F32),
        ],
        scratch_shapes=[pltpu.VMEM((PEERS, 64, 128), F32)],
        compiler_params=params(),
        cost_estimate=cost(1_000_000, 1_000_000),
        name="filter_inner",
    )(lower_cut, upper_bound, orbitals, potential, rot_tile)
    received = lax.all_to_all(send, "orb", split_axis=0, concat_axis=0, tiled=True)

    filtered, *sends_outer = pl.pallas_call(
        outer_kernel,
        grid=(ORBS, 2),
        in_specs=[SMEM] * 3 + [VMEM] * 5 + [ANY],
        out_specs=[pl.BlockSpec((1, 4) + plane, lambda i, s: (i, 3 * s, 0, 0))] + [VMEM] * PEERS,
        out_shape=[filtered_shape] + [jax.ShapeDtypeStruct((256, 128), F32)] * PEERS,
        scratch_shapes=[
            pltpu.VMEM((4,) + plane, F32),
            pltpu.VMEM((PEERS, 32, 128), F32),
        ],
        input_output_aliases={8: 0},
        compiler_params=params(),
        cost_estimate=cost(400_000_000_000, 400_000_000),
        name="filter_outer",
    )(mine, lower_cut, upper_bound, orbitals, potential, stored, low, high, filtered)
    received_outer = regroup(sends_outer)

    weights = received[:, 256, : ORBS * NCOL]
    rotated_shape = jax.ShapeDtypeStruct((NCOL, PLANES, 4, COLS), F32)
    rotated = pl.pallas_call(
        rotate_inner_kernel,
        grid=(2,),
        in_specs=[SMEM, VMEM],
        out_specs=pl.BlockSpec((NCOL, 4, 4, COLS), lambda u: (0, 1 + u, 0, 0)),
        out_shape=rotated_shape,
        compiler_params=params(),
        cost_estimate=cost(8_000_000, 1_600_000),
        name="rotate_inner",
    )(weights, received)
    rotated = pl.pallas_call(
        rotate_outer_kernel,
        grid=(2,),
        in_specs=[SMEM, SMEM] + [VMEM] * PEERS + [ANY],
        out_specs=pl.BlockSpec((NCOL, 4, 4, COLS), lambda u: (0, 3 * u, 0, 0)),
        out_shape=rotated_shape,
        input_output_aliases={PEERS + 2: 0},
        compiler_params=params(),
        cost_estimate=cost(8_000_000, 1_600_000),
        name="rotate_outer",
    )(mine, weights, *received_outer, rotated)
    return (filtered, rotated)


def solution(mesh):
    in_specs = (P("orb", "grid", None, None), P("grid", None, None), P(), P(), P("orb", None))
    out_specs = (P("orb", "grid", None, None), P(None, "grid", "orb", None))
    return jax.shard_map(body, mesh=mesh, in_specs=in_specs, out_specs=out_specs, check_vma=False)
```

```python
import jax
import jax.numpy as jnp
from jax import lax
from jax.experimental import pallas as pl
from jax.experimental.pallas import tpu as pltpu
from jax.sharding import PartitionSpec as P

W0, W1, W2 = -5.0 / 2.0, 4.0 / 3.0, -1.0 / 12.0
F32 = jnp.float32
ORBS, PLANES, ROWS, COLS = 4, 16, 32, 256
REACH = 4
PEERS, NCOL = 8, 16
RUN = 8
DIRECT = 2
LIMIT = 20 * 1024 * 1024
ORDER = (1, 2, 4, 5, 6, 7, 3, 0)


def coefficients(lower_ref, upper_ref):
    middle = (upper_ref[0] + lower_ref[0]) * 0.5
    inverse = 1.0 / ((upper_ref[0] - lower_ref[0]) * 0.5)
    return (-1.5 * W0 - middle) * inverse, inverse, -0.5 * W1 * inverse


def scaled_hamilton(planes, local, coef):
    base, inverse, near = coef
    below2, below1, f, above1, above2 = planes
    s1 = below1 + above1
    s2 = below2 + above2
    s1 = s1 + (pltpu.roll(f, 1, 0) + pltpu.roll(f, ROWS - 1, 0))
    s2 = s2 + (pltpu.roll(f, 2, 0) + pltpu.roll(f, ROWS - 2, 0))
    s1 = s1 + (pltpu.roll(f, 1, 1) + pltpu.roll(f, COLS - 1, 1))
    s2 = s2 + (pltpu.roll(f, 2, 1) + pltpu.roll(f, COLS - 2, 1))
    return f * (base + inverse * local) + near * (s1 + (W2 / W1) * s2)


def first_planes(count, source, local, store, coef):
    def step(p, carry):
        store(p, scaled_hamilton([source(p + d) for d in range(5)], local(p), coef))
        return carry

    lax.fori_loop(0, count, step, 0, unroll=2)


def filtered_plane(q, first, original, local, coef):
    g = scaled_hamilton([first(q + d) for d in range(5)], local, coef)
    return 2.0 * g - original


def pack_pair(mine, slots_ref, row, g0, g1):
    low = lax.broadcasted_iota(jnp.int32, (8, 128), 0) < 4
    for k in range(ROWS // 8):
        for h in range(COLS // 128):
            a = g0[8 * k : 8 * k + 8, 128 * h : 128 * h + 128]
            b = g1[8 * k : 8 * k + 8, 128 * h : 128 * h + 128]
            at = slice(row + 8 * h, row + 8 * h + 8)
            slots_ref[jnp.bitwise_xor(mine, 2 * k), at, :] = jnp.where(low, a, pltpu.roll(b, 4, 0))
            slots_ref[jnp.bitwise_xor(mine, 2 * k + 1), at, :] = jnp.where(
                low, pltpu.roll(a, 4, 0), b
            )


def inner_kernel(
    lower_ref, upper_ref, orb_ref, pot_ref, rot_ref, out_ref, first_ref, send_ref, slots_ref
):
    coef = coefficients(lower_ref, upper_ref)
    orbital = pl.program_id(0)

    def store(p, value):
        first_ref[0, p] = value

    first_planes(12, lambda p: orb_ref[0, p], lambda p: pot_ref[p + 2], store, coef)
    for t in range(4):
        pair = []
        for q in (2 * t, 2 * t + 1):
            g = filtered_plane(
                q, lambda p: first_ref[0, p], orb_ref[0, q + 4], pot_ref[q + 4], coef
            )
            out_ref[0, q + 4] = g
            pair.append(g)
        pack_pair(0, slots_ref, t * 16, *pair)
    for slot in range(PEERS):
        send_ref[slot, pl.ds(pl.multiple_of(orbital * 64, 64), 64), :] = slots_ref[slot]
        send_ref[slot, 256:264, :] = rot_ref[...]


def outer_kernel(
    mine_ref, position_ref, lower_ref, upper_ref, orb_ref, pot_ref, stored_ref, low_ref, high_ref,
    far_direct_ref, far_relayed_ref, _, *rest,
):
    out_ref, sends, (halo_ref, halo_pot_ref, fresh_ref, slots_ref) = rest[0], rest[1:-4], rest[-4:]
    coef = coefficients(lower_ref, upper_ref)
    mine, position = mine_ref[0], position_ref[0]
    i, side = pl.program_id(0), pl.program_id(1)
    far = ((side == 0) & (position == 0)) | ((side == 1) & (position == RUN - 1))
    at = REACH * i + jnp.where(i < DIRECT, 0, 2)

    def take(condition, ref, start):
        @pl.when(condition)
        def _():
            halo_ref[...] = ref[pl.ds(start, REACH)]

    def take_pot(condition, ref, start):
        @pl.when(condition)
        def _():
            halo_pot_ref[...] = ref[start : start + 2]

    take(~far & (side == 0), low_ref, at)
    take(~far & (side == 1), high_ref, at)
    take(far & (i < DIRECT), far_direct_ref, jnp.minimum(at, REACH * (DIRECT - 1)))
    take(far & (i >= DIRECT), far_relayed_ref, jnp.maximum(at - REACH * DIRECT, 0))
    take_pot(~far & (side == 0), low_ref, REACH * DIRECT)
    take_pot(~far & (side == 1), high_ref, REACH * DIRECT)
    take_pot(far, far_relayed_ref, 0)

    def filter_side(raw, local, first, original, own_local):
        for p in range(4):
            fresh_ref[p] = scaled_hamilton([raw(p + d) for d in range(5)], local(p), coef)
        for t in range(2):
            pair = []
            for q in (2 * t, 2 * t + 1):
                g = filtered_plane(q, first, original(q), own_local(q), coef)
                out_ref[0, q] = g
                pair.append(g)
            pack_pair(mine, slots_ref, t * 16, *pair)

    @pl.when(side == 0)
    def _():
        filter_side(
            lambda p: halo_ref[p] if p < 4 else orb_ref[0, p - 4],
            lambda p: halo_pot_ref[p] if p < 2 else pot_ref[p - 2],
            lambda p: fresh_ref[p] if p < 4 else stored_ref[0, p - 4],
            lambda q: orb_ref[0, q],
            lambda q: pot_ref[q],
        )

    @pl.when(side == 1)
    def _():
        filter_side(
            lambda p: orb_ref[0, p] if p < 4 else halo_ref[p - 4],
            lambda p: pot_ref[14 + p] if p < 2 else halo_pot_ref[p - 2],
            lambda p: stored_ref[0, p] if p < 4 else fresh_ref[p - 4],
            lambda q: orb_ref[0, q],
            lambda q: pot_ref[12 + q],
        )

    rows = pl.ds(pl.multiple_of((2 * i + side) * 32, 32), 32)
    for slot, send_ref in enumerate(sends):
        send_ref[rows, :] = slots_ref[slot]


def rotate_tiles(u, tile, weight, out_ref):
    width = 8
    for first in range(0, NCOL, width):
        sums = [jnp.zeros((8, 128), F32)] * (4 * width)
        for slot in range(PEERS):
            for i in range(ORBS):
                rows = [pl.multiple_of(i * 64 + u * 32 + 8 * n, 8) for n in range(4)]
                values = [tile(slot, pl.ds(row, 8)) for row in rows]
                for j in range(width):
                    factor = weight(slot, i * NCOL + first + j)
                    for n in range(4):
                        sums[4 * j + n] = sums[4 * j + n] + factor * values[n]
        for j in range(width):
            for n in range(4):
                t, h = divmod(n, 2)
                columns = slice(128 * h, 128 * h + 128)
                out_ref[first + j, 2 * t, :, columns] = sums[4 * j + n][0:4]
                out_ref[first + j, 2 * t + 1, :, columns] = sums[4 * j + n][4:8]


def rotate_inner_kernel(rot_ref, recv_ref, out_ref):
    rotate_tiles(
        pl.program_id(0),
        lambda slot, rows: recv_ref[slot, rows, :],
        lambda slot, n: rot_ref[slot, n],
        out_ref,
    )


def rotate_outer_kernel(mine_ref, rot_ref, *rest):
    received, out_ref, mine = rest[:PEERS], rest[-1], mine_ref[0]
    rotate_tiles(
        pl.program_id(0),
        lambda slot, rows: received[slot][rows, :],
        lambda slot, n: rot_ref[jnp.bitwise_xor(mine, ORDER[slot]), n],
        out_ref,
    )


SMEM = pl.BlockSpec(memory_space=pltpu.SMEM)
VMEM = pl.BlockSpec(memory_space=pltpu.VMEM)
ANY = pl.BlockSpec(memory_space=pl.ANY)


def params():
    return pltpu.CompilerParams(vmem_limit_bytes=LIMIT)


def cost(flops, moved):
    return pl.CostEstimate(flops=flops, bytes_accessed=moved, transcendentals=0)


def body(orbitals, potential, lower_cut, upper_bound, rotation):
    count = lax.axis_size("grid")
    plane = (ROWS, COLS)
    position = lax.axis_index("grid").astype(jnp.int32) % RUN
    ring = [(g, (g + 1) % count) for g in range(count)]
    near = [(g, h) for g, h in ring if g % RUN != RUN - 1]
    ends = [(g, h) for g, h in ring if g % RUN == RUN - 1]
    inwards = [(g, g - 1) for g, _ in ends] + [(h, h + 1) for _, h in ends]
    across = [(g - 1, h) for g, h in ends] + [(h + 1, g) for g, h in ends]

    def swapped(pairs):
        return [(target, source) for source, target in pairs]

    def packed(first_plane, first_local):
        own = orbitals[:, first_plane : first_plane + REACH].reshape((ORBS * REACH,) + plane)
        local = potential[first_local : first_local + 2]
        half = REACH * DIRECT
        return jnp.concatenate([own[:half], local, own[half:]], axis=0)

    top, bottom = packed(PLANES - REACH, PLANES - 2), packed(0, 0)
    to_far = jnp.where(position == RUN - 1, top, bottom)
    direct = REACH * DIRECT
    relay = lax.ppermute(to_far[direct:], "grid", inwards)
    far_relayed = lax.ppermute(relay, "grid", across)
    far_direct = lax.ppermute(to_far[:direct], "grid", ends + swapped(ends))
    low = lax.ppermute(top, "grid", near)
    high = lax.ppermute(bottom, "grid", swapped(near))

    orb_hbm = pltpu.with_memory_space_constraint(orbitals, pltpu.HBM)
    pot_hbm = pltpu.with_memory_space_constraint(potential, pltpu.HBM)
    rot_tile = jnp.pad(rotation.reshape(1, ORBS * NCOL), ((0, 7), (0, 128 - ORBS * NCOL)))
    mine = lax.axis_index("orb").astype(jnp.int32).reshape(1)
    filtered_shape = pltpu.HBM((ORBS, PLANES) + plane, F32)

    def regroup(sends):
        return [
            lax.ppermute(sends[k], "orb", [(o, o ^ k) for o in range(PEERS)]) if k else sends[k]
            for k in ORDER
        ]

    filtered, stored, send = pl.pallas_call(
        inner_kernel,
        grid=(ORBS,),
        in_specs=[
            SMEM,
            SMEM,
            pl.BlockSpec((1, PLANES) + plane, lambda i: (i, 0, 0, 0)),
            pl.BlockSpec((PLANES,) + plane, lambda i: (0, 0, 0)),
            pl.BlockSpec((8, 128), lambda i: (0, 0)),
        ],
        out_specs=[
            pl.BlockSpec((1, PLANES) + plane, lambda i: (i, 0, 0, 0)),
            pl.BlockSpec((1, 12) + plane, lambda i: (i, 0, 0, 0)),
            pl.BlockSpec((PEERS, 264, 128), lambda i: (0, 0, 0)),
        ],
        out_shape=[
            filtered_shape,
            pltpu.HBM((ORBS, 12) + plane, F32),
            pltpu.HBM((PEERS, 264, 128), F32),
        ],
        scratch_shapes=[pltpu.VMEM((PEERS, 64, 128), F32)],
        compiler_params=params(),
        cost_estimate=cost(1_000_000, 1_000_000),
        name="filter_inner",
    )(lower_cut, upper_bound, orb_hbm, pot_hbm, rot_tile)
    received = lax.all_to_all(send, "orb", split_axis=0, concat_axis=0, tiled=True)
    stored = pltpu.with_memory_space_constraint(stored, pltpu.HBM)

    filtered, *sends_outer = pl.pallas_call(
        outer_kernel,
        grid=(ORBS, 2),
        in_specs=[SMEM] * 4
        + [
            pl.BlockSpec((1, 4) + plane, lambda i, s: (i, 3 * s, 0, 0)),
            pl.BlockSpec((PLANES,) + plane, lambda i, s: (0, 0, 0)),
            pl.BlockSpec((1, 4) + plane, lambda i, s: (i, 2 * s, 0, 0)),
        ]
        + [VMEM] * 4
        + [ANY],
        out_specs=[pl.BlockSpec((1, 4) + plane, lambda i, s: (i, 3 * s, 0, 0))] + [VMEM] * PEERS,
        out_shape=[filtered_shape] + [jax.ShapeDtypeStruct((256, 128), F32)] * PEERS,
        scratch_shapes=[
            pltpu.VMEM((4,) + plane, F32),
            pltpu.VMEM((2,) + plane, F32),
            pltpu.VMEM((4,) + plane, F32),
            pltpu.VMEM((PEERS, 32, 128), F32),
        ],
        input_output_aliases={11: 0},
        compiler_params=params(),
        cost_estimate=cost(400_000_000_000, 400_000_000),
        name="filter_outer",
    )(
        mine, position.reshape(1), lower_cut, upper_bound, orb_hbm, pot_hbm, stored,
        low, high, far_direct, far_relayed, filtered,
    )
    received_outer = regroup(sends_outer)

    weights = received[:, 256, : ORBS * NCOL]
    rotated_shape = jax.ShapeDtypeStruct((NCOL, PLANES, 4, COLS), F32)
    rotated = pl.pallas_call(
        rotate_inner_kernel,
        grid=(2,),
        in_specs=[SMEM, VMEM],
        out_specs=pl.BlockSpec((NCOL, 4, 4, COLS), lambda u: (0, 1 + u, 0, 0)),
        out_shape=rotated_shape,
        compiler_params=params(),
        cost_estimate=cost(8_000_000, 1_600_000),
        name="rotate_inner",
    )(weights, received)
    rotated = pl.pallas_call(
        rotate_outer_kernel,
        grid=(2,),
        in_specs=[SMEM, SMEM] + [VMEM] * PEERS + [ANY],
        out_specs=pl.BlockSpec((NCOL, 4, 4, COLS), lambda u: (0, 3 * u, 0, 0)),
        out_shape=rotated_shape,
        input_output_aliases={PEERS + 2: 0},
        compiler_params=params(),
        cost_estimate=cost(8_000_000, 1_600_000),
        name="rotate_outer",
    )(mine, weights, *received_outer, rotated)
    return (filtered, rotated)


def solution(mesh):
    in_specs = (P("orb", "grid", None, None), P("grid", None, None), P(), P(), P("orb", None))
    out_specs = (P("orb", "grid", None, None), P(None, "grid", "orb", None))
    return jax.shard_map(body, mesh=mesh, in_specs=in_specs, out_specs=out_specs, check_vma=False)
```

```python
import jax
import jax.numpy as jnp
from jax import lax
from jax.experimental import pallas as pl
from jax.experimental.pallas import tpu as pltpu
from jax.sharding import PartitionSpec as P

W0, W1, W2 = -5.0 / 2.0, 4.0 / 3.0, -1.0 / 12.0
F32 = jnp.float32
ORBS, PLANES, ROWS, COLS = 4, 16, 32, 256
REACH = 4
PEERS, NCOL = 8, 16
LIMIT = 20 * 1024 * 1024
SOON, LAST = (1, 2, 4, 5, 0), (6, 7, 3)


def coefficients(lower, upper):
    middle = (upper + lower) * 0.5
    inverse = 1.0 / ((upper - lower) * 0.5)
    return (-1.5 * W0 - middle) * inverse, inverse, -0.5 * W1 * inverse


def scaled_hamilton(planes, local, coef):
    base, inverse, near = coef
    below2, below1, f, above1, above2 = planes
    s1 = below1 + above1
    s2 = below2 + above2
    s1 = s1 + (pltpu.roll(f, 1, 0) + pltpu.roll(f, ROWS - 1, 0))
    s2 = s2 + (pltpu.roll(f, 2, 0) + pltpu.roll(f, ROWS - 2, 0))
    s1 = s1 + (pltpu.roll(f, 1, 1) + pltpu.roll(f, COLS - 1, 1))
    s2 = s2 + (pltpu.roll(f, 2, 1) + pltpu.roll(f, COLS - 2, 1))
    return f * (base + inverse * local) + near * (s1 + (W2 / W1) * s2)


def first_planes(count, source, local, store, coef):
    def step(p, carry):
        store(p, scaled_hamilton([source(p + d) for d in range(5)], local(p), coef))
        return carry

    lax.fori_loop(0, count, step, 0, unroll=2)


def filtered_plane(q, first, original, local, coef):
    g = scaled_hamilton([first(q + d) for d in range(5)], local, coef)
    return 2.0 * g - original


def pack_pair(mine, slots_ref, row, g0, g1):
    low = lax.broadcasted_iota(jnp.int32, (8, 128), 0) < 4
    for k in range(ROWS // 8):
        for h in range(COLS // 128):
            a = g0[8 * k : 8 * k + 8, 128 * h : 128 * h + 128]
            b = g1[8 * k : 8 * k + 8, 128 * h : 128 * h + 128]
            at = slice(row + 8 * h, row + 8 * h + 8)
            slots_ref[jnp.bitwise_xor(mine, 2 * k), at, :] = jnp.where(low, a, pltpu.roll(b, 4, 0))
            slots_ref[jnp.bitwise_xor(mine, 2 * k + 1), at, :] = jnp.where(
                low, pltpu.roll(a, 4, 0), b
            )


def inner_kernel(
    lower_ref, upper_ref, orb_ref, pot_ref, rot_ref, out_ref, first_ref, send_ref, slots_ref
):
    coef = coefficients(lower_ref[0], upper_ref[0])
    orbital = pl.program_id(0)

    def store(p, value):
        first_ref[0, p] = value

    first_planes(12, lambda p: orb_ref[0, p], lambda p: pot_ref[p + 2], store, coef)
    for t in range(4):
        pair = []
        for q in (2 * t, 2 * t + 1):
            g = filtered_plane(
                q, lambda p: first_ref[0, p], orb_ref[0, q + 4], pot_ref[q + 4], coef
            )
            out_ref[0, q + 4] = g
            pair.append(g)
        pack_pair(0, slots_ref, t * 16, *pair)
    for slot in range(PEERS):
        send_ref[slot, pl.ds(pl.multiple_of(orbital * 64, 64), 64), :] = slots_ref[slot]
        send_ref[slot, 256:264, :] = rot_ref[...]


def outer_kernel(
    mine_ref, lower_ref, upper_ref, orb_ref, pot_ref, stored_ref, low_ref, high_ref, _, *rest
):
    out_ref, sends, (fresh_ref, slots_ref) = rest[0], rest[1:-2], rest[-2:]
    coef = coefficients(lower_ref[0], upper_ref[0])
    mine, i, side = mine_ref[0], pl.program_id(0), pl.program_id(1)
    halo = REACH * i

    def filter_side(raw, local, first, original, own_local):
        for p in range(4):
            fresh_ref[p] = scaled_hamilton([raw(p + d) for d in range(5)], local(p), coef)
        for t in range(2):
            pair = []
            for q in (2 * t, 2 * t + 1):
                g = filtered_plane(q, first, original(q), own_local(q), coef)
                out_ref[0, q] = g
                pair.append(g)
            pack_pair(mine, slots_ref, t * 16, *pair)

    @pl.when(side == 0)
    def _():
        filter_side(
            lambda p: low_ref[halo + p] if p < 4 else orb_ref[0, p - 4],
            lambda p: low_ref[ORBS * REACH + p] if p < 2 else pot_ref[p - 2],
            lambda p: fresh_ref[p] if p < 4 else stored_ref[0, p - 4],
            lambda q: orb_ref[0, q],
            lambda q: pot_ref[q],
        )

    @pl.when(side == 1)
    def _():
        filter_side(
            lambda p: orb_ref[0, p] if p < 4 else high_ref[halo + p - 4],
            lambda p: pot_ref[14 + p] if p < 2 else high_ref[ORBS * REACH + p - 2],
            lambda p: stored_ref[0, p] if p < 4 else fresh_ref[p - 4],
            lambda q: orb_ref[0, q],
            lambda q: pot_ref[12 + q],
        )

    rows = pl.ds(pl.multiple_of((2 * i + side) * 32, 32), 32)
    for slot, send_ref in enumerate(sends):
        send_ref[rows, :] = slots_ref[slot]


def rotate_tiles(u, slots, tile, weight, start, finish):
    width = 8
    for first in range(0, NCOL, width):
        sums = [start(first + m // 4, m % 4) for m in range(4 * width)]
        for slot in slots:
            for i in range(ORBS):
                rows = [pl.multiple_of(i * 64 + u * 32 + 8 * n, 8) for n in range(4)]
                values = [tile(slot, pl.ds(row, 8)) for row in rows]
                for j in range(width):
                    factor = weight(slot, i * NCOL + first + j)
                    for n in range(4):
                        sums[4 * j + n] = sums[4 * j + n] + factor * values[n]
        for m in range(4 * width):
            finish(first + m // 4, m % 4, sums[m])


def zero_start(j, n):
    return jnp.zeros((8, 128), F32)


def write_to(out_ref):
    def finish(j, n, value):
        t, h = divmod(n, 2)
        columns = slice(128 * h, 128 * h + 128)
        out_ref[j, 2 * t, :, columns] = value[0:4]
        out_ref[j, 2 * t + 1, :, columns] = value[4:8]

    return finish


def rotate_inner_kernel(rot_ref, recv_ref, out_ref):
    rotate_tiles(
        pl.program_id(0),
        range(PEERS),
        lambda slot, rows: recv_ref[slot, rows, :],
        lambda slot, n: rot_ref[slot, n],
        zero_start,
        write_to(out_ref),
    )


def rotate_soon_kernel(mine_ref, rot_ref, *rest):
    received, sums_ref, mine, u = rest[:-1], rest[-1], mine_ref[0], pl.program_id(0)

    def finish(j, n, value):
        sums_ref[u, 4 * j + n] = value

    rotate_tiles(
        u,
        range(len(SOON)),
        lambda slot, rows: received[slot][rows, :],
        lambda slot, n: rot_ref[jnp.bitwise_xor(mine, SOON[slot]), n],
        zero_start,
        finish,
    )


def rotate_last_kernel(mine_ref, rot_ref, sums_ref, *rest):
    received, out_ref, mine, u = rest[:-2], rest[-1], mine_ref[0], pl.program_id(0)
    rotate_tiles(
        u,
        range(len(LAST)),
        lambda slot, rows: received[slot][rows, :],
        lambda slot, n: rot_ref[jnp.bitwise_xor(mine, LAST[slot]), n],
        lambda j, n: sums_ref[u, 4 * j + n],
        write_to(out_ref),
    )


SMEM = pl.BlockSpec(memory_space=pltpu.SMEM)
VMEM = pl.BlockSpec(memory_space=pltpu.VMEM)
ANY = pl.BlockSpec(memory_space=pl.ANY)


def params():
    return pltpu.CompilerParams(vmem_limit_bytes=LIMIT)


def cost(flops, moved):
    return pl.CostEstimate(flops=flops, bytes_accessed=moved, transcendentals=0)


def body(orbitals, potential, lower_cut, upper_bound, rotation):
    count = lax.axis_size("grid")
    forward = [(i, (i + 1) % count) for i in range(count)]
    backward = [(target, source) for source, target in forward]
    plane = (ROWS, COLS)

    def packed(first_plane, first_local):
        own = orbitals[:, first_plane : first_plane + REACH].reshape((ORBS * REACH,) + plane)
        return jnp.concatenate([own, potential[first_local : first_local + 2]], axis=0)

    low = lax.ppermute(packed(PLANES - REACH, PLANES - 2), "grid", forward)
    high = lax.ppermute(packed(0, 0), "grid", backward)

    orb_hbm = pltpu.with_memory_space_constraint(orbitals, pltpu.HBM)
    pot_hbm = pltpu.with_memory_space_constraint(potential, pltpu.HBM)
    lower, upper = lower_cut, upper_bound
    rot_tile = jnp.pad(rotation.reshape(1, ORBS * NCOL), ((0, 7), (0, 128 - ORBS * NCOL)))
    mine = lax.axis_index("orb").astype(jnp.int32).reshape(1)
    filtered_shape = pltpu.HBM((ORBS, PLANES) + plane, F32)

    def regroup(sends):
        return [
            lax.ppermute(sends[k], "orb", [(o, o ^ k) for o in range(PEERS)]) if k else sends[k]
            for k in SOON + LAST
        ]

    filtered, stored, send = pl.pallas_call(
        inner_kernel,
        grid=(ORBS,),
        in_specs=[
            VMEM,
            VMEM,
            pl.BlockSpec((1, PLANES) + plane, lambda i: (i, 0, 0, 0)),
            pl.BlockSpec((PLANES,) + plane, lambda i: (0, 0, 0)),
            pl.BlockSpec((8, 128), lambda i: (0, 0)),
        ],
        out_specs=[
            pl.BlockSpec((1, PLANES) + plane, lambda i: (i, 0, 0, 0)),
            pl.BlockSpec((1, 12) + plane, lambda i: (i, 0, 0, 0)),
            pl.BlockSpec((PEERS, 264, 128), lambda i: (0, 0, 0)),
        ],
        out_shape=[
            filtered_shape,
            pltpu.HBM((ORBS, 12) + plane, F32),
            pltpu.HBM((PEERS, 264, 128), F32),
        ],
        scratch_shapes=[pltpu.VMEM((PEERS, 64, 128), F32)],
        compiler_params=params(),
        cost_estimate=cost(1_000_000, 1_000_000),
        name="filter_inner",
    )(lower, upper, orb_hbm, pot_hbm, rot_tile)
    received = lax.all_to_all(send, "orb", split_axis=0, concat_axis=0, tiled=True)
    stored = pltpu.with_memory_space_constraint(stored, pltpu.HBM)

    filtered, *sends_outer = pl.pallas_call(
        outer_kernel,
        grid=(ORBS, 2),
        in_specs=[SMEM, VMEM, VMEM]
        + [
            pl.BlockSpec((1, 4) + plane, lambda i, s: (i, 3 * s, 0, 0)),
            pl.BlockSpec((PLANES,) + plane, lambda i, s: (0, 0, 0)),
            pl.BlockSpec((1, 4) + plane, lambda i, s: (i, 2 * s, 0, 0)),
        ]
        + [VMEM] * 2
        + [ANY],
        out_specs=[pl.BlockSpec((1, 4) + plane, lambda i, s: (i, 3 * s, 0, 0))] + [VMEM] * PEERS,
        out_shape=[filtered_shape] + [jax.ShapeDtypeStruct((256, 128), F32)] * PEERS,
        scratch_shapes=[
            pltpu.VMEM((4,) + plane, F32),
            pltpu.VMEM((PEERS, 32, 128), F32),
        ],
        input_output_aliases={8: 0},
        compiler_params=params(),
        cost_estimate=cost(400_000_000_000, 400_000_000),
        name="filter_outer",
    )(mine, lower, upper, orb_hbm, pot_hbm, stored, low, high, filtered)
    received_outer = regroup(sends_outer)

    weights = received[:, 256, : ORBS * NCOL]
    rotated_shape = jax.ShapeDtypeStruct((NCOL, PLANES, 4, COLS), F32)
    rotated = pl.pallas_call(
        rotate_inner_kernel,
        grid=(2,),
        in_specs=[SMEM, VMEM],
        out_specs=pl.BlockSpec((NCOL, 4, 4, COLS), lambda u: (0, 1 + u, 0, 0)),
        out_shape=rotated_shape,
        compiler_params=params(),
        cost_estimate=cost(8_000_000, 1_600_000),
        name="rotate_inner",
    )(weights, received)
    sums = pl.pallas_call(
        rotate_soon_kernel,
        grid=(2,),
        in_specs=[SMEM, SMEM] + [VMEM] * len(SOON),
        out_specs=VMEM,
        out_shape=jax.ShapeDtypeStruct((2, 4 * NCOL, 8, 128), F32),
        compiler_params=params(),
        cost_estimate=cost(5_000_000, 1_100_000),
        name="rotate_soon",
    )(mine, weights, *received_outer[: len(SOON)])
    rotated = pl.pallas_call(
        rotate_last_kernel,
        grid=(2,),
        in_specs=[SMEM, SMEM, VMEM] + [VMEM] * len(LAST) + [ANY],
        out_specs=pl.BlockSpec((NCOL, 4, 4, COLS), lambda u: (0, 3 * u, 0, 0)),
        out_shape=rotated_shape,
        input_output_aliases={len(LAST) + 3: 0},
        compiler_params=params(),
        cost_estimate=cost(3_000_000, 1_100_000),
        name="rotate_last",
    )(mine, weights, sums, *received_outer[len(SOON) :], rotated)
    return (filtered, rotated)


def solution(mesh):
    in_specs = (P("orb", "grid", None, None), P("grid", None, None), P(), P(), P("orb", None))
    out_specs = (P("orb", "grid", None, None), P(None, "grid", "orb", None))
    return jax.shard_map(body, mesh=mesh, in_specs=in_specs, out_specs=out_specs, check_vma=False)
```

```python
import jax
import jax.numpy as jnp
from jax import lax
from jax.experimental import pallas as pl
from jax.experimental.pallas import tpu as pltpu
from jax.sharding import PartitionSpec as P

W0, W1, W2 = -5.0 / 2.0, 4.0 / 3.0, -1.0 / 12.0
F32 = jnp.float32
ORBS, PLANES, ROWS, COLS = 4, 16, 32, 256
REACH = 4
PEERS, NCOL = 8, 16
LIMIT = 20 * 1024 * 1024
SOON, LAST = (1, 2, 4, 5, 0), (6, 7, 3)


def coefficients(lower, upper):
    middle = (upper + lower) * 0.5
    inverse = 1.0 / ((upper - lower) * 0.5)
    return (-1.5 * W0 - middle) * inverse, inverse, -0.5 * W1 * inverse


def scaled_hamilton(planes, local, coef):
    base, inverse, near = coef
    below2, below1, f, above1, above2 = planes
    s1 = below1 + above1
    s2 = below2 + above2
    s1 = s1 + (pltpu.roll(f, 1, 0) + pltpu.roll(f, ROWS - 1, 0))
    s2 = s2 + (pltpu.roll(f, 2, 0) + pltpu.roll(f, ROWS - 2, 0))
    s1 = s1 + (pltpu.roll(f, 1, 1) + pltpu.roll(f, COLS - 1, 1))
    s2 = s2 + (pltpu.roll(f, 2, 1) + pltpu.roll(f, COLS - 2, 1))
    return f * (base + inverse * local) + near * (s1 + (W2 / W1) * s2)


def first_planes(count, source, local, store, coef):
    def step(p, carry):
        store(p, scaled_hamilton([source(p + d) for d in range(5)], local(p), coef))
        return carry

    lax.fori_loop(0, count, step, 0, unroll=4)


def filtered_plane(q, first, original, local, coef):
    g = scaled_hamilton([first(q + d) for d in range(5)], local, coef)
    return 2.0 * g - original


def pack_pair(mine, slots_ref, row, g0, g1):
    low = lax.broadcasted_iota(jnp.int32, (8, 128), 0) < 4
    for k in range(ROWS // 8):
        for h in range(COLS // 128):
            a = g0[8 * k : 8 * k + 8, 128 * h : 128 * h + 128]
            b = g1[8 * k : 8 * k + 8, 128 * h : 128 * h + 128]
            at = slice(row + 8 * h, row + 8 * h + 8)
            slots_ref[jnp.bitwise_xor(mine, 2 * k), at, :] = jnp.where(low, a, pltpu.roll(b, 4, 0))
            slots_ref[jnp.bitwise_xor(mine, 2 * k + 1), at, :] = jnp.where(
                low, pltpu.roll(a, 4, 0), b
            )


def inner_kernel(
    lower_ref, upper_ref, orb_ref, pot_ref, rot_ref, out_ref, first_ref, send_ref, slots_ref
):
    coef = coefficients(lower_ref[0], upper_ref[0])
    orbital = pl.program_id(0)

    def store(p, value):
        first_ref[0, p] = value

    first_planes(12, lambda p: orb_ref[0, p], lambda p: pot_ref[p + 2], store, coef)
    for t in range(4):
        pair = []
        for q in (2 * t, 2 * t + 1):
            g = filtered_plane(
                q, lambda p: first_ref[0, p], orb_ref[0, q + 4], pot_ref[q + 4], coef
            )
            out_ref[0, q + 4] = g
            pair.append(g)
        pack_pair(0, slots_ref, t * 16, *pair)
    for slot in range(PEERS):
        send_ref[slot, pl.ds(pl.multiple_of(orbital * 64, 64), 64), :] = slots_ref[slot]
        send_ref[slot, 256:264, :] = rot_ref[...]


def outer_kernel(
    mine_ref, lower_ref, upper_ref, orb_ref, pot_ref, stored_ref, low_ref, high_ref, _, *rest
):
    out_ref, sends, (fresh_ref, slots_ref) = rest[0], rest[1:-2], rest[-2:]
    coef = coefficients(lower_ref[0], upper_ref[0])
    mine, i, side = mine_ref[0], pl.program_id(0), pl.program_id(1)
    halo = REACH * i

    def filter_side(raw, local, first, original, own_local):
        for p in range(4):
            fresh_ref[p] = scaled_hamilton([raw(p + d) for d in range(5)], local(p), coef)
        for t in range(2):
            pair = []
            for q in (2 * t, 2 * t + 1):
                g = filtered_plane(q, first, original(q), own_local(q), coef)
                out_ref[0, q] = g
                pair.append(g)
            pack_pair(mine, slots_ref, t * 16, *pair)

    @pl.when(side == 0)
    def _():
        filter_side(
            lambda p: low_ref[halo + p] if p < 4 else orb_ref[0, p - 4],
            lambda p: low_ref[ORBS * REACH + p] if p < 2 else pot_ref[p - 2],
            lambda p: fresh_ref[p] if p < 4 else stored_ref[0, p - 4],
            lambda q: orb_ref[0, q],
            lambda q: pot_ref[q],
        )

    @pl.when(side == 1)
    def _():
        filter_side(
            lambda p: orb_ref[0, p] if p < 4 else high_ref[halo + p - 4],
            lambda p: pot_ref[14 + p] if p < 2 else high_ref[ORBS * REACH + p - 2],
            lambda p: stored_ref[0, p] if p < 4 else fresh_ref[p - 4],
            lambda q: orb_ref[0, q],
            lambda q: pot_ref[12 + q],
        )

    rows = pl.ds(pl.multiple_of((2 * i + side) * 32, 32), 32)
    for slot, send_ref in enumerate(sends):
        send_ref[rows, :] = slots_ref[slot]


def rotate_tiles(u, slots, tile, weight, start, finish):
    width = 8
    for first in range(0, NCOL, width):
        sums = [start(first + m // 4, m % 4) for m in range(4 * width)]
        for slot in slots:
            for i in range(ORBS):
                rows = [pl.multiple_of(i * 64 + u * 32 + 8 * n, 8) for n in range(4)]
                values = [tile(slot, pl.ds(row, 8)) for row in rows]
                for j in range(width):
                    factor = weight(slot, i * NCOL + first + j)
                    for n in range(4):
                        sums[4 * j + n] = sums[4 * j + n] + factor * values[n]
        for m in range(4 * width):
            finish(first + m // 4, m % 4, sums[m])


def zero_start(j, n):
    return jnp.zeros((8, 128), F32)


def write_to(out_ref):
    def finish(j, n, value):
        t, h = divmod(n, 2)
        columns = slice(128 * h, 128 * h + 128)
        out_ref[j, 2 * t, :, columns] = value[0:4]
        out_ref[j, 2 * t + 1, :, columns] = value[4:8]

    return finish


def rotate_inner_kernel(rot_ref, recv_ref, out_ref):
    rotate_tiles(
        pl.program_id(0),
        range(PEERS),
        lambda slot, rows: recv_ref[slot, rows, :],
        lambda slot, n: rot_ref[slot, n],
        zero_start,
        write_to(out_ref),
    )


def rotate_soon_kernel(mine_ref, rot_ref, *rest):
    received, sums_ref, mine, u = rest[:-2], rest[-1], mine_ref[0], pl.program_id(0)

    def finish(j, n, value):
        sums_ref[u, 4 * j + n] = value

    rotate_tiles(
        u,
        range(len(SOON)),
        lambda slot, rows: received[slot][rows, :],
        lambda slot, n: rot_ref[jnp.bitwise_xor(mine, SOON[slot]), n],
        zero_start,
        finish,
    )


def rotate_last_kernel(mine_ref, rot_ref, sums_ref, *rest):
    received, out_ref, mine, u = rest[:-2], rest[-1], mine_ref[0], pl.program_id(0)
    rotate_tiles(
        u,
        range(len(LAST)),
        lambda slot, rows: received[slot][rows, :],
        lambda slot, n: rot_ref[jnp.bitwise_xor(mine, LAST[slot]), n],
        lambda j, n: sums_ref[u, 4 * j + n],
        write_to(out_ref),
    )


SMEM = pl.BlockSpec(memory_space=pltpu.SMEM)
VMEM = pl.BlockSpec(memory_space=pltpu.VMEM)
ANY = pl.BlockSpec(memory_space=pl.ANY)


def params():
    return pltpu.CompilerParams(vmem_limit_bytes=LIMIT)


def cost(flops, moved):
    return pl.CostEstimate(flops=flops, bytes_accessed=moved, transcendentals=0)


def body(orbitals, potential, lower_cut, upper_bound, rotation):
    count = lax.axis_size("grid")
    forward = [(i, (i + 1) % count) for i in range(count)]
    backward = [(target, source) for source, target in forward]
    plane = (ROWS, COLS)

    def packed(first_plane, first_local):
        own = orbitals[:, first_plane : first_plane + REACH].reshape((ORBS * REACH,) + plane)
        return jnp.concatenate([own, potential[first_local : first_local + 2]], axis=0)

    low = lax.ppermute(packed(PLANES - REACH, PLANES - 2), "grid", forward)
    high = lax.ppermute(packed(0, 0), "grid", backward)

    orb_hbm = pltpu.with_memory_space_constraint(orbitals, pltpu.HBM)
    pot_hbm = pltpu.with_memory_space_constraint(potential, pltpu.HBM)
    lower, upper = lower_cut, upper_bound
    rot_tile = jnp.pad(rotation.reshape(1, ORBS * NCOL), ((0, 7), (0, 128 - ORBS * NCOL)))
    mine = lax.axis_index("orb").astype(jnp.int32).reshape(1)
    filtered_shape = pltpu.HBM((ORBS, PLANES) + plane, F32)

    def regroup(sends):
        return [
            lax.ppermute(sends[k], "orb", [(o, o ^ k) for o in range(PEERS)]) if k else sends[k]
            for k in SOON + LAST
        ]

    filtered, stored, send = pl.pallas_call(
        inner_kernel,
        grid=(ORBS,),
        in_specs=[
            VMEM,
            VMEM,
            pl.BlockSpec((1, PLANES) + plane, lambda i: (i, 0, 0, 0)),
            pl.BlockSpec((PLANES,) + plane, lambda i: (0, 0, 0)),
            pl.BlockSpec((8, 128), lambda i: (0, 0)),
        ],
        out_specs=[
            pl.BlockSpec((1, PLANES) + plane, lambda i: (i, 0, 0, 0)),
            pl.BlockSpec((1, 12) + plane, lambda i: (i, 0, 0, 0)),
            pl.BlockSpec((PEERS, 264, 128), lambda i: (0, 0, 0)),
        ],
        out_shape=[
            filtered_shape,
            pltpu.HBM((ORBS, 12) + plane, F32),
            pltpu.HBM((PEERS, 264, 128), F32),
        ],
        scratch_shapes=[pltpu.VMEM((PEERS, 64, 128), F32)],
        compiler_params=params(),
        cost_estimate=cost(1_000_000, 1_000_000),
        name="filter_inner",
    )(lower, upper, orb_hbm, pot_hbm, rot_tile)
    received = lax.all_to_all(send, "orb", split_axis=0, concat_axis=0, tiled=True)
    stored = pltpu.with_memory_space_constraint(stored, pltpu.HBM)

    filtered, *sends_outer = pl.pallas_call(
        outer_kernel,
        grid=(ORBS, 2),
        in_specs=[SMEM, VMEM, VMEM]
        + [
            pl.BlockSpec((1, 4) + plane, lambda i, s: (i, 3 * s, 0, 0)),
            pl.BlockSpec((PLANES,) + plane, lambda i, s: (0, 0, 0)),
            pl.BlockSpec((1, 4) + plane, lambda i, s: (i, 2 * s, 0, 0)),
        ]
        + [VMEM] * 2
        + [ANY],
        out_specs=[pl.BlockSpec((1, 4) + plane, lambda i, s: (i, 3 * s, 0, 0))] + [VMEM] * PEERS,
        out_shape=[filtered_shape] + [jax.ShapeDtypeStruct((256, 128), F32)] * PEERS,
        scratch_shapes=[
            pltpu.VMEM((4,) + plane, F32),
            pltpu.VMEM((PEERS, 32, 128), F32),
        ],
        input_output_aliases={8: 0},
        compiler_params=params(),
        cost_estimate=cost(400_000_000_000, 400_000_000),
        name="filter_outer",
    )(mine, lower, upper, orb_hbm, pot_hbm, stored, low, high, filtered)
    received_outer = regroup(sends_outer)

    weights = received[:, 256, : ORBS * NCOL]
    rotated_shape = pltpu.HBM((NCOL, PLANES, 4, COLS), F32)
    rotated = pl.pallas_call(
        rotate_inner_kernel,
        grid=(2,),
        in_specs=[SMEM, VMEM],
        out_specs=pl.BlockSpec((NCOL, 4, 4, COLS), lambda u: (0, 1 + u, 0, 0)),
        out_shape=rotated_shape,
        compiler_params=params(),
        cost_estimate=cost(8_000_000, 1_600_000),
        name="rotate_inner",
    )(weights, received)
    rotated = pltpu.with_memory_space_constraint(rotated, pltpu.HBM)
    sums = pl.pallas_call(
        rotate_soon_kernel,
        grid=(2,),
        in_specs=[SMEM, SMEM] + [VMEM] * len(SOON) + [ANY],
        out_specs=VMEM,
        out_shape=jax.ShapeDtypeStruct((2, 4 * NCOL, 8, 128), F32),
        compiler_params=params(),
        cost_estimate=cost(5_000_000, 1_100_000),
        name="rotate_soon",
    )(mine, weights, *received_outer[: len(SOON)], rotated)
    rotated = pl.pallas_call(
        rotate_last_kernel,
        grid=(2,),
        in_specs=[SMEM, SMEM, VMEM] + [VMEM] * len(LAST) + [ANY],
        out_specs=pl.BlockSpec((NCOL, 4, 4, COLS), lambda u: (0, 3 * u, 0, 0)),
        out_shape=rotated_shape,
        input_output_aliases={len(LAST) + 3: 0},
        compiler_params=params(),
        cost_estimate=cost(3_000_000, 1_100_000),
        name="rotate_last",
    )(mine, weights, sums, *received_outer[len(SOON) :], rotated)
    return (filtered, rotated)


def solution(mesh):
    in_specs = (P("orb", "grid", None, None), P("grid", None, None), P(), P(), P("orb", None))
    out_specs = (P("orb", "grid", None, None), P(None, "grid", "orb", None))
    return jax.shard_map(body, mesh=mesh, in_specs=in_specs, out_specs=out_specs, check_vma=False)
```

```python
import jax
import jax.numpy as jnp
from jax import lax
from jax.experimental import pallas as pl
from jax.experimental.pallas import tpu as pltpu
from jax.sharding import PartitionSpec as P

W0, W1, W2 = -5.0 / 2.0, 4.0 / 3.0, -1.0 / 12.0
F32 = jnp.float32
ORBS, PLANES, ROWS, COLS = 4, 16, 32, 256
REACH = 4
PEERS, NCOL = 8, 16
LIMIT = 20 * 1024 * 1024
SOON, LAST = (1, 2, 4, 5, 0), (6, 7, 3)


def coefficients(lower, upper):
    middle = (upper + lower) * 0.5
    inverse = 1.0 / ((upper - lower) * 0.5)
    return (-1.5 * W0 - middle) * inverse, inverse, -0.5 * W1 * inverse


def scaled_hamilton(planes, local, coef):
    base, inverse, near = coef
    below2, below1, f, above1, above2 = planes
    s1 = below1 + above1
    s2 = below2 + above2
    s1 = s1 + (pltpu.roll(f, 1, 0) + pltpu.roll(f, ROWS - 1, 0))
    s2 = s2 + (pltpu.roll(f, 2, 0) + pltpu.roll(f, ROWS - 2, 0))
    s1 = s1 + (pltpu.roll(f, 1, 1) + pltpu.roll(f, COLS - 1, 1))
    s2 = s2 + (pltpu.roll(f, 2, 1) + pltpu.roll(f, COLS - 2, 1))
    return f * (base + inverse * local) + near * (s1 + (W2 / W1) * s2)


def first_planes(count, source, local, store, coef):
    def step(p, carry):
        store(p, scaled_hamilton([source(p + d) for d in range(5)], local(p), coef))
        return carry

    lax.fori_loop(0, count, step, 0, unroll=True)


def filtered_plane(q, first, original, local, coef):
    g = scaled_hamilton([first(q + d) for d in range(5)], local, coef)
    return 2.0 * g - original


def pack_pair(mine, slots_ref, row, g0, g1):
    low = lax.broadcasted_iota(jnp.int32, (8, 128), 0) < 4
    for k in range(ROWS // 8):
        for h in range(COLS // 128):
            a = g0[8 * k : 8 * k + 8, 128 * h : 128 * h + 128]
            b = g1[8 * k : 8 * k + 8, 128 * h : 128 * h + 128]
            at = slice(row + 8 * h, row + 8 * h + 8)
            slots_ref[jnp.bitwise_xor(mine, 2 * k), at, :] = jnp.where(low, a, pltpu.roll(b, 4, 0))
            slots_ref[jnp.bitwise_xor(mine, 2 * k + 1), at, :] = jnp.where(
                low, pltpu.roll(a, 4, 0), b
            )


def inner_kernel(
    lower_ref, upper_ref, orb_ref, pot_ref, rot_ref, out_ref, first_ref, send_ref, slots_ref
):
    coef = coefficients(lower_ref[0], upper_ref[0])
    orbital = pl.program_id(0)

    def store(p, value):
        first_ref[0, p] = value

    first_planes(12, lambda p: orb_ref[0, p], lambda p: pot_ref[p + 2], store, coef)
    for t in range(4):
        pair = []
        for q in (2 * t, 2 * t + 1):
            g = filtered_plane(
                q, lambda p: first_ref[0, p], orb_ref[0, q + 4], pot_ref[q + 4], coef
            )
            out_ref[0, q + 4] = g
            pair.append(g)
        pack_pair(0, slots_ref, t * 16, *pair)
    for slot in range(PEERS):
        send_ref[slot, pl.ds(pl.multiple_of(orbital * 64, 64), 64), :] = slots_ref[slot]
        send_ref[slot, 256:264, :] = rot_ref[...]


def outer_kernel(
    mine_ref, lower_ref, upper_ref, orb_ref, pot_ref, stored_ref, low_ref, high_ref, _, *rest
):
    out_ref, sends, (fresh_ref, slots_ref) = rest[0], rest[1:-2], rest[-2:]
    coef = coefficients(lower_ref[0], upper_ref[0])
    mine, i, side = mine_ref[0], pl.program_id(0), pl.program_id(1)
    halo = REACH * i

    def filter_side(raw, local, first, original, own_local):
        for p in range(4):
            fresh_ref[p] = scaled_hamilton([raw(p + d) for d in range(5)], local(p), coef)
        for t in range(2):
            pair = []
            for q in (2 * t, 2 * t + 1):
                g = filtered_plane(q, first, original(q), own_local(q), coef)
                out_ref[0, q] = g
                pair.append(g)
            pack_pair(mine, slots_ref, t * 16, *pair)

    @pl.when(side == 0)
    def _():
        filter_side(
            lambda p: low_ref[halo + p] if p < 4 else orb_ref[0, p - 4],
            lambda p: low_ref[ORBS * REACH + p] if p < 2 else pot_ref[p - 2],
            lambda p: fresh_ref[p] if p < 4 else stored_ref[0, p - 4],
            lambda q: orb_ref[0, q],
            lambda q: pot_ref[q],
        )

    @pl.when(side == 1)
    def _():
        filter_side(
            lambda p: orb_ref[0, p] if p < 4 else high_ref[halo + p - 4],
            lambda p: pot_ref[14 + p] if p < 2 else high_ref[ORBS * REACH + p - 2],
            lambda p: stored_ref[0, p] if p < 4 else fresh_ref[p - 4],
            lambda q: orb_ref[0, q],
            lambda q: pot_ref[12 + q],
        )

    rows = pl.ds(pl.multiple_of((2 * i + side) * 32, 32), 32)
    for slot, send_ref in enumerate(sends):
        send_ref[rows, :] = slots_ref[slot]


def rotate_tiles(u, slots, tile, weight, start, finish):
    width = 8
    for first in range(0, NCOL, width):
        sums = [start(first + m // 4, m % 4) for m in range(4 * width)]
        for slot in slots:
            for i in range(ORBS):
                rows = [pl.multiple_of(i * 64 + u * 32 + 8 * n, 8) for n in range(4)]
                values = [tile(slot, pl.ds(row, 8)) for row in rows]
                for j in range(width):
                    factor = weight(slot, i * NCOL + first + j)
                    for n in range(4):
                        sums[4 * j + n] = sums[4 * j + n] + factor * values[n]
        for m in range(4 * width):
            finish(first + m // 4, m % 4, sums[m])


def zero_start(j, n):
    return jnp.zeros((8, 128), F32)


def write_to(out_ref):
    def finish(j, n, value):
        t, h = divmod(n, 2)
        columns = slice(128 * h, 128 * h + 128)
        out_ref[j, 2 * t, :, columns] = value[0:4]
        out_ref[j, 2 * t + 1, :, columns] = value[4:8]

    return finish


def rotate_inner_kernel(rot_ref, recv_ref, out_ref):
    rotate_tiles(
        pl.program_id(0),
        range(PEERS),
        lambda slot, rows: recv_ref[slot, rows, :],
        lambda slot, n: rot_ref[slot, n],
        zero_start,
        write_to(out_ref),
    )


def rotate_soon_kernel(mine_ref, rot_ref, *rest):
    received, sums_ref, mine, u = rest[:-2], rest[-1], mine_ref[0], pl.program_id(0)

    def finish(j, n, value):
        sums_ref[u, 4 * j + n] = value

    rotate_tiles(
        u,
        range(len(SOON)),
        lambda slot, rows: received[slot][rows, :],
        lambda slot, n: rot_ref[jnp.bitwise_xor(mine, SOON[slot]), n],
        zero_start,
        finish,
    )


def rotate_last_kernel(mine_ref, rot_ref, sums_ref, *rest):
    received, out_ref, mine, u = rest[:-2], rest[-1], mine_ref[0], pl.program_id(0)
    rotate_tiles(
        u,
        range(len(LAST)),
        lambda slot, rows: received[slot][rows, :],
        lambda slot, n: rot_ref[jnp.bitwise_xor(mine, LAST[slot]), n],
        lambda j, n: sums_ref[u, 4 * j + n],
        write_to(out_ref),
    )


SMEM = pl.BlockSpec(memory_space=pltpu.SMEM)
VMEM = pl.BlockSpec(memory_space=pltpu.VMEM)
ANY = pl.BlockSpec(memory_space=pl.ANY)


def params():
    return pltpu.CompilerParams(vmem_limit_bytes=LIMIT)


def cost(flops, moved):
    return pl.CostEstimate(flops=flops, bytes_accessed=moved, transcendentals=0)


def body(orbitals, potential, lower_cut, upper_bound, rotation):
    count = lax.axis_size("grid")
    forward = [(i, (i + 1) % count) for i in range(count)]
    backward = [(target, source) for source, target in forward]
    plane = (ROWS, COLS)

    def packed(first_plane, first_local):
        own = orbitals[:, first_plane : first_plane + REACH].reshape((ORBS * REACH,) + plane)
        return jnp.concatenate([own, potential[first_local : first_local + 2]], axis=0)

    low = lax.ppermute(packed(PLANES - REACH, PLANES - 2), "grid", forward)
    high = lax.ppermute(packed(0, 0), "grid", backward)

    orb_hbm = pltpu.with_memory_space_constraint(orbitals, pltpu.HBM)
    pot_hbm = pltpu.with_memory_space_constraint(potential, pltpu.HBM)
    lower, upper = lower_cut, upper_bound
    rot_tile = jnp.pad(rotation.reshape(1, ORBS * NCOL), ((0, 7), (0, 128 - ORBS * NCOL)))
    mine = lax.axis_index("orb").astype(jnp.int32).reshape(1)
    filtered_shape = pltpu.HBM((ORBS, PLANES) + plane, F32)

    def regroup(sends):
        return [
            lax.ppermute(sends[k], "orb", [(o, o ^ k) for o in range(PEERS)]) if k else sends[k]
            for k in SOON + LAST
        ]

    filtered, stored, send = pl.pallas_call(
        inner_kernel,
        grid=(ORBS,),
        in_specs=[
            VMEM,
            VMEM,
            pl.BlockSpec((1, PLANES) + plane, lambda i: (i, 0, 0, 0)),
            pl.BlockSpec((PLANES,) + plane, lambda i: (0, 0, 0)),
            pl.BlockSpec((8, 128), lambda i: (0, 0)),
        ],
        out_specs=[
            pl.BlockSpec((1, PLANES) + plane, lambda i: (i, 0, 0, 0)),
            pl.BlockSpec((1, 12) + plane, lambda i: (i, 0, 0, 0)),
            pl.BlockSpec((PEERS, 264, 128), lambda i: (0, 0, 0)),
        ],
        out_shape=[
            filtered_shape,
            pltpu.HBM((ORBS, 12) + plane, F32),
            pltpu.HBM((PEERS, 264, 128), F32),
        ],
        scratch_shapes=[pltpu.VMEM((PEERS, 64, 128), F32)],
        compiler_params=params(),
        cost_estimate=cost(1_000_000, 1_000_000),
        name="filter_inner",
    )(lower, upper, orb_hbm, pot_hbm, rot_tile)
    received = lax.all_to_all(send, "orb", split_axis=0, concat_axis=0, tiled=True)
    stored = pltpu.with_memory_space_constraint(stored, pltpu.HBM)

    filtered, *sends_outer = pl.pallas_call(
        outer_kernel,
        grid=(ORBS, 2),
        in_specs=[SMEM, VMEM, VMEM]
        + [
            pl.BlockSpec((1, 4) + plane, lambda i, s: (i, 3 * s, 0, 0)),
            pl.BlockSpec((PLANES,) + plane, lambda i, s: (0, 0, 0)),
            pl.BlockSpec((1, 4) + plane, lambda i, s: (i, 2 * s, 0, 0)),
        ]
        + [VMEM] * 2
        + [ANY],
        out_specs=[pl.BlockSpec((1, 4) + plane, lambda i, s: (i, 3 * s, 0, 0))] + [VMEM] * PEERS,
        out_shape=[filtered_shape] + [jax.ShapeDtypeStruct((256, 128), F32)] * PEERS,
        scratch_shapes=[
            pltpu.VMEM((4,) + plane, F32),
            pltpu.VMEM((PEERS, 32, 128), F32),
        ],
        input_output_aliases={8: 0},
        compiler_params=params(),
        cost_estimate=cost(400_000_000_000, 400_000_000),
        name="filter_outer",
    )(mine, lower, upper, orb_hbm, pot_hbm, stored, low, high, filtered)
    received_outer = regroup(sends_outer)

    weights = received[:, 256, : ORBS * NCOL]
    rotated_shape = pltpu.HBM((NCOL, PLANES, 4, COLS), F32)
    rotated = pl.pallas_call(
        rotate_inner_kernel,
        grid=(2,),
        in_specs=[SMEM, VMEM],
        out_specs=pl.BlockSpec((NCOL, 4, 4, COLS), lambda u: (0, 1 + u, 0, 0)),
        out_shape=rotated_shape,
        compiler_params=params(),
        cost_estimate=cost(8_000_000, 1_600_000),
        name="rotate_inner",
    )(weights, received)
    rotated = pltpu.with_memory_space_constraint(rotated, pltpu.HBM)
    sums = pl.pallas_call(
        rotate_soon_kernel,
        grid=(2,),
        in_specs=[SMEM, SMEM] + [VMEM] * len(SOON) + [ANY],
        out_specs=VMEM,
        out_shape=jax.ShapeDtypeStruct((2, 4 * NCOL, 8, 128), F32),
        compiler_params=params(),
        cost_estimate=cost(5_000_000, 1_100_000),
        name="rotate_soon",
    )(mine, weights, *received_outer[: len(SOON)], rotated)
    rotated = pl.pallas_call(
        rotate_last_kernel,
        grid=(2,),
        in_specs=[SMEM, SMEM, VMEM] + [VMEM] * len(LAST) + [ANY],
        out_specs=pl.BlockSpec((NCOL, 4, 4, COLS), lambda u: (0, 3 * u, 0, 0)),
        out_shape=rotated_shape,
        input_output_aliases={len(LAST) + 3: 0},
        compiler_params=params(),
        cost_estimate=cost(3_000_000, 1_100_000),
        name="rotate_last",
    )(mine, weights, sums, *received_outer[len(SOON) :], rotated)
    return (filtered, rotated)


def solution(mesh):
    in_specs = (P("orb", "grid", None, None), P("grid", None, None), P(), P(), P("orb", None))
    out_specs = (P("orb", "grid", None, None), P(None, "grid", "orb", None))
    return jax.shard_map(body, mesh=mesh, in_specs=in_specs, out_specs=out_specs, check_vma=False)
```
